32 devices in a mesh: ao: 8 (over z, core), chol: 4 (over y, x).
Axes of the slice: x: 2, y: 2, z: 4, core: 2. Of those that a mesh axis runs over, the one named last changes fastest.
Arguments:
- cholesky: bfloat16 [8, 3072, 3072], P('chol', 'ao'), may hold values from -2.109375 to 2.109375
- coeffs: bfloat16 [3072, 128], P('ao'), may hold values from -0.109375 to 0.109375
Outputs:
- pair_integrals: bfloat16 [16384, 16384], P('ao', 'chol')
The draws below stay inside these ranges and needn't reach their ends.
All inputs are finite; a program needn't handle non-finite values.
Results may differ from the reference program's by a relative error of at most 0.007.
Values may be sent and summed in bfloat16 or wider, within the bound.
No kernel may reach another device: no remote copies, remote signals or barrier semaphores. Data moves between devices by JAX's collectives and lax.ppermute only.
A program may use at most 64 MiB of HBM per device.

```python
import jax
import jax.numpy as jnp
from jax import lax

NAO = 3072
IMP = 128
VECS = 8
PAIRS = 16384
N_AO = 8


def block_scale(stream_key, extent, split, low, high):
    level = 1.0
    for dim, shards_of in split:
        steps = jax.random.uniform(jax.random.fold_in(jax.random.fold_in(stream_key, 6), dim), (shards_of,), jnp.float32, low / len(split), high / len(split))
        level = level * jnp.repeat(jnp.exp(steps), extent[dim] // shards_of).reshape((-1,) + (1,) * (len(extent) - 1 - dim))
    return level


def normal_values(stream_key, extent, scale, reach, shards=(), kind=jnp.bfloat16):
    level = block_scale(stream_key, extent, shards, -0.22, 0.18) if shards else 1.0
    values = jax.random.normal(stream_key, extent, jnp.float32) * scale * level
    return jnp.minimum(jnp.maximum(values, -reach), reach).astype(kind)


def setup_inputs(seed: int = 0) -> dict:
    key_list = jax.random.split(jax.random.key(seed), 3)
    cholesky = normal_values(key_list[0], (VECS, NAO, NAO), (VECS ** -0.5), 2.109375, ((0, 4), (1, 8)))
    coeffs = normal_values(key_list[1], (NAO, IMP), NAO ** -0.5, 0.109375, ((0, 8),))
    return {"cholesky": cholesky, "coeffs": coeffs}


def reference(cholesky, coeffs):
    def project(vector):
        product = jnp.dot(vector, coeffs, preferred_element_type=jnp.float32).astype(jnp.bfloat16)
        summed = jnp.dot(coeffs.T, product, preferred_element_type=jnp.float32)
        return summed.astype(jnp.bfloat16).reshape(-1)

    pair_vectors = lax.map(project, cholesky)
    block_rows = pair_vectors.reshape(VECS, N_AO, PAIRS // N_AO).transpose(1, 0, 2)

    def gram(rows_block):
        return jnp.dot(rows_block.T, pair_vectors, preferred_element_type=jnp.float32).astype(jnp.bfloat16)

    return lax.map(gram, block_rows).reshape(PAIRS, PAIRS)
```

```python
import functools

import jax
import jax.numpy as jnp
from jax import lax
from jax.experimental import pallas as pl
from jax.experimental.pallas import tpu as pltpu
from jax.sharding import Mesh, PartitionSpec as P

CORES = 2
AO = ("z", "core")
SWAP = [(0, 1), (1, 0)]


def pick(array, index, size, dim):
    return lax.dynamic_slice_in_dim(array, index * size, size, dim)


def flip(array, axis, step):
    count = lax.axis_size(axis)
    return lax.ppermute(array, axis, [(d, d ^ step) for d in range(count)])


def project_kernel(nz, left_ref, *refs):
    held, out_ref = refs[:nz], refs[-1]
    z, core = lax.axis_index("z"), lax.axis_index("core")
    for p in range(out_ref.shape[0]):
        total = refs[nz][p] if len(refs) > nz + 1 else 0.0
        for s in range(nz):
            total += lax.dot_general(
                left_ref[p, z ^ s, core if left_ref.shape[2] > 1 else 0],
                held[s][...],
                (((0,), (0,)), ((), ())),
                preferred_element_type=jnp.float32,
            )
        out_ref[p] = total


def project(left, held, *before, flops):
    vec_dev, nz, _, rows, orbitals = left.shape
    whole = pl.BlockSpec(memory_space=pltpu.VMEM)
    return pl.pallas_call(
        functools.partial(project_kernel, nz),
        out_shape=jax.ShapeDtypeStruct((vec_dev, orbitals, orbitals), jnp.float32),
        in_specs=[whole] * (1 + nz + len(before)),
        out_specs=whole,
        compiler_params=pltpu.CompilerParams(vmem_limit_bytes=32 << 20),
        cost_estimate=pl.CostEstimate(
            flops=flops, bytes_accessed=flops // 1000, transcendentals=0
        ),
    )(left, *held, *before)


def head_kernel(slab, row_ref, col_ref, head_ref, flipped_ref):
    flipped_ref[...] = row_ref[...].astype(jnp.float32).T.astype(flipped_ref.dtype)
    for n in range(head_ref.shape[1] // slab):
        at = pl.ds(n * slab, slab)
        head_ref[:, at] = jnp.dot(
            flipped_ref[...], col_ref[:, at], preferred_element_type=jnp.float32
        ).astype(head_ref.dtype)


def rest_kernel(slab, side, head_ref, flipped_ref, col_ref, out_ref, block, sems):
    heads = head_ref.shape[1] // slab
    own, per = sems.shape[0] // CORES, side // slab
    core = lax.axis_index("core")

    def write(source, n, t):
        s, owner = t % own, (core + t // own) % CORES
        to = (s // per * CORES + owner) * side + s % per * slab
        return pltpu.make_async_copy(
            source.at[:, pl.ds(pl.multiple_of(n * slab, slab), slab)],
            out_ref.at[:, pl.ds(pl.multiple_of(to, slab), slab)],
            sems.at[t],
        )

    for n in range(heads):
        write(head_ref, n, n).start()

    rest = sems.shape[0] - heads

    @pl.loop(0, rest, unroll=3 if rest % 3 == 0 else 1)
    def _(n):
        at = pl.ds(pl.multiple_of(n * slab, slab), slab)
        block[:, at] = jnp.dot(
            flipped_ref[...], col_ref[:, at], preferred_element_type=jnp.float32
        ).astype(block.dtype)
        write(block, n, n + heads).start()

    for n in range(heads):
        write(head_ref, n, n).wait()

    @pl.loop(0, rest)
    def _(n):
        write(block, n, n + heads).wait()


def head_product(row_part, col_part, slab):
    vecs, rows = row_part.shape
    width = slab * max(1, col_part.shape[1] // slab // 2)
    whole = pl.BlockSpec(memory_space=pltpu.VMEM)
    return pl.pallas_call(
        functools.partial(head_kernel, slab),
        out_shape=(
            jax.ShapeDtypeStruct((rows, width), jnp.bfloat16),
            jax.ShapeDtypeStruct((rows, vecs), jnp.bfloat16),
        ),
        in_specs=[whole] * 2,
        out_specs=(whole, whole),
        compiler_params=pltpu.CompilerParams(vmem_limit_bytes=24 << 20),
        cost_estimate=pl.CostEstimate(
            flops=2 * vecs * rows * width, bytes_accessed=2 * rows * width, transcendentals=0
        ),
    )(row_part, col_part)


def rest_product(head, flipped, col_rest, side, slab):
    rows, vecs = flipped.shape
    width = col_rest.shape[1]
    cols = head.shape[1] + width
    whole = pl.BlockSpec(memory_space=pltpu.VMEM)
    return pl.pallas_call(
        functools.partial(rest_kernel, slab, side),
        out_shape=jax.ShapeDtypeStruct((rows, cols), jnp.bfloat16),
        in_specs=[whole] * 3,
        out_specs=pl.BlockSpec(memory_space=pl.ANY),
        scratch_shapes=[
            pltpu.VMEM((rows, width), jnp.bfloat16),
            pltpu.SemaphoreType.DMA((cols // slab,)),
        ],
        compiler_params=pltpu.CompilerParams(vmem_limit_bytes=32 << 20),
        cost_estimate=pl.CostEstimate(
            flops=2 * vecs * rows * width, bytes_accessed=2 * rows * cols, transcendentals=0
        ),
    )(head, flipped, col_rest)


def body(cholesky, coeffs):
    vec_dev, rows, nao = cholesky.shape
    orbitals = coeffs.shape[1]
    nz, n_chol = lax.axis_size("z"), lax.axis_size("chol")
    z, core, chol = lax.axis_index("z"), lax.axis_index("core"), lax.axis_index("chol")

    held = [coeffs] + [flip(coeffs, "z", s) for s in range(1, nz)]

    left = jnp.einsum("ri,prk->pki", coeffs, cholesky, preferred_element_type=jnp.float32)
    left = left.astype(jnp.bfloat16).reshape(vec_dev, nz, CORES, rows, orbitals)
    give = lax.dynamic_slice_in_dim(left, 1 - core, 1, 2)
    got = lax.ppermute(give, "core", SWAP)
    partial = project(left, held, flops=10**11)
    partial = project(got, held, partial, flops=2 * got.size * orbitals)

    span = orbitals // (nz * CORES)
    partial = partial.reshape(vec_dev, nz, CORES, span, orbitals)
    total = lax.dynamic_index_in_dim(partial, core, 2, keepdims=False)
    total += lax.ppermute(
        lax.dynamic_index_in_dim(partial, 1 - core, 2, keepdims=False), "core", SWAP
    )
    rounded = total.astype(jnp.bfloat16)
    for s in range(1, nz):
        total += flip(rounded, "z", s).astype(jnp.float32)
    values = total.astype(jnp.bfloat16)

    wide = nz // n_chol
    row_out = pick(values, z, 1, 1)
    seen = [jnp.concatenate([row_out, pick(values, chol, wide, 1)], 1)]
    for s in range(n_chol - 1, 0, -1):
        seen.append(flip(jnp.concatenate([row_out, pick(values, chol ^ s, wide, 1)], 1), "chol", s))
    seen = jnp.concatenate(seen, 0)
    vecs = seen.shape[0]
    row_part, col_own = seen[:, :1].reshape(vecs, -1), seen[:, 1:].reshape(vecs, -1)

    col_got = lax.ppermute(seen[:, 1:], "core", SWAP).reshape(vecs, -1)
    side = span * orbitals
    slab = min(side, 512)
    head, flipped = head_product(row_part, col_own, slab)
    col_rest = jnp.concatenate([col_own[:, head.shape[1] :], col_got], 1)
    return rest_product(head, flipped, col_rest, side, slab)


def solution(mesh):
    n_ao, n_chol = mesh.shape["ao"], mesh.shape["chol"]
    split = Mesh(mesh.devices.reshape(n_ao // CORES, CORES, n_chol), (*AO, "chol"))
    placed = (P("chol", AO, None), P(AO, None))
    return jax.shard_map(
        body, mesh=split, in_specs=placed, out_specs=P(AO, "chol"), check_vma=False
    )
```

```python
import functools

import jax
import jax.numpy as jnp
from jax import lax
from jax.experimental import pallas as pl
from jax.experimental.pallas import tpu as pltpu
from jax.sharding import Mesh, PartitionSpec as P

CORES = 2
AO = ("z", "core")
SWAP = [(0, 1), (1, 0)]


def pick(array, index, size, dim):
    return lax.dynamic_slice_in_dim(array, index * size, size, dim)


def flip(array, axis, step):
    count = lax.axis_size(axis)
    return lax.ppermute(array, axis, [(d, d ^ step) for d in range(count)])


def project_kernel(nz, left_ref, *refs):
    held, out_ref = refs[:nz], refs[-1]
    z, core = lax.axis_index("z"), lax.axis_index("core")
    for p in range(out_ref.shape[0]):
        total = refs[nz][p] if len(refs) > nz + 1 else 0.0
        for s in range(nz):
            total += lax.dot_general(
                left_ref[p, z ^ s, core if left_ref.shape[2] > 1 else 0],
                held[s][...],
                (((0,), (0,)), ((), ())),
                preferred_element_type=jnp.float32,
            )
        out_ref[p] = total


def project(left, held, *before, flops):
    vec_dev, nz, _, rows, orbitals = left.shape
    whole = pl.BlockSpec(memory_space=pltpu.VMEM)
    return pl.pallas_call(
        functools.partial(project_kernel, nz),
        out_shape=jax.ShapeDtypeStruct((vec_dev, orbitals, orbitals), jnp.float32),
        in_specs=[whole] * (1 + nz + len(before)),
        out_specs=whole,
        compiler_params=pltpu.CompilerParams(vmem_limit_bytes=32 << 20),
        cost_estimate=pl.CostEstimate(
            flops=flops, bytes_accessed=flops // 1000, transcendentals=0
        ),
    )(left, *held, *before)


BLOCKS = 4


def block_product(flipped_ref, col_ref, into_ref, n, size):
    at = pl.ds(pl.multiple_of(n * size, size), size)
    return at, jnp.dot(
        flipped_ref[at, :], col_ref[...], preferred_element_type=jnp.float32
    ).astype(into_ref.dtype)


def head_kernel(size, row_ref, col_ref, head_ref, flipped_ref):
    flipped_ref[...] = row_ref[...].astype(jnp.float32).T.astype(flipped_ref.dtype)
    for n in range(head_ref.shape[0] // size):
        at, made = block_product(flipped_ref, col_ref, head_ref, n, size)
        head_ref[at, :] = made


def rest_kernel(side, size, head_ref, flipped_ref, own_ref, got_ref, out_ref, own, other, sems):
    core = lax.axis_index("core")
    parts = own_ref.shape[1] // side
    heads = head_ref.shape[0] // size

    def writes(source, n, to, owner):
        for part in range(parts):
            yield pltpu.make_async_copy(
                source.at[pl.ds(pl.multiple_of(n * size, size), size), pl.ds(part * side, side)],
                out_ref.at[
                    pl.ds(pl.multiple_of(to * size, size), size),
                    pl.ds(pl.multiple_of((part * CORES + owner) * side, side), side),
                ],
                sems.at[owner, to, part],
            )

    def each(act):
        for n in range(heads):
            for copy in writes(head_ref, n, n, core):
                act(copy)

        @pl.loop(0, BLOCKS - heads, unroll=act is start)
        def _(n):
            if act is start:
                to = n + heads
                made = block_product(flipped_ref, own_ref, own, to, size)[1]
                own[pl.ds(pl.multiple_of(n * size, size), size), :] = made
            for copy in writes(own, n, n + heads, core):
                act(copy)

        @pl.loop(0, BLOCKS, unroll=act is start)
        def _(n):
            if act is start:
                at, made = block_product(flipped_ref, got_ref, other, n, size)
                other[at, :] = made
            for copy in writes(other, n, n, 1 - core):
                act(copy)

    def start(copy):
        copy.start()

    each(start)
    each(lambda copy: copy.wait())


def head_product(row_part, col_part):
    vecs, rows = row_part.shape
    width = col_part.shape[1]
    whole = pl.BlockSpec(memory_space=pltpu.VMEM)
    return pl.pallas_call(
        functools.partial(head_kernel, rows // BLOCKS),
        out_shape=(
            jax.ShapeDtypeStruct((rows // 2, width), jnp.bfloat16),
            jax.ShapeDtypeStruct((rows, vecs), jnp.bfloat16),
        ),
        in_specs=[whole] * 2,
        out_specs=(whole, whole),
        compiler_params=pltpu.CompilerParams(vmem_limit_bytes=24 << 20),
        cost_estimate=pl.CostEstimate(
            flops=vecs * rows * width, bytes_accessed=rows * width, transcendentals=0
        ),
    )(row_part, col_part)


def rest_product(head, flipped, col_own, col_got, side):
    rows, vecs = flipped.shape
    width = col_own.shape[1]
    whole = pl.BlockSpec(memory_space=pltpu.VMEM)
    return pl.pallas_call(
        functools.partial(rest_kernel, side, rows // BLOCKS),
        out_shape=jax.ShapeDtypeStruct((rows, 2 * width), jnp.bfloat16),
        in_specs=[whole] * 4,
        out_specs=pl.BlockSpec(memory_space=pl.ANY),
        scratch_shapes=[
            pltpu.VMEM((rows - head.shape[0], width), jnp.bfloat16),
            pltpu.VMEM((rows, width), jnp.bfloat16),
            pltpu.SemaphoreType.DMA((CORES, BLOCKS, width // side)),
        ],
        compiler_params=pltpu.CompilerParams(vmem_limit_bytes=32 << 20),
        cost_estimate=pl.CostEstimate(
            flops=3 * vecs * rows * width, bytes_accessed=4 * rows * width, transcendentals=0
        ),
    )(head, flipped, col_own, col_got)


def body(cholesky, coeffs):
    vec_dev, rows, nao = cholesky.shape
    orbitals = coeffs.shape[1]
    nz, n_chol = lax.axis_size("z"), lax.axis_size("chol")
    z, core, chol = lax.axis_index("z"), lax.axis_index("core"), lax.axis_index("chol")

    held = [coeffs] + [flip(coeffs, "z", s) for s in range(1, nz)]

    left = jnp.einsum("ri,prk->pki", coeffs, cholesky, preferred_element_type=jnp.float32)
    left = left.astype(jnp.bfloat16).reshape(vec_dev, nz, CORES, rows, orbitals)
    give = lax.dynamic_slice_in_dim(left, 1 - core, 1, 2)
    got = lax.ppermute(give, "core", SWAP)
    partial = project(left, held, flops=10**11)
    partial = project(got, held, partial, flops=2 * got.size * orbitals)

    span = orbitals // (nz * CORES)
    partial = partial.reshape(vec_dev, nz, CORES, span, orbitals)
    total = lax.dynamic_index_in_dim(partial, core, 2, keepdims=False)
    total += lax.ppermute(
        lax.dynamic_index_in_dim(partial, 1 - core, 2, keepdims=False), "core", SWAP
    )
    rounded = total.astype(jnp.bfloat16)
    for s in range(1, nz):
        total += flip(rounded, "z", s).astype(jnp.float32)
    values = total.astype(jnp.bfloat16)

    wide = nz // n_chol
    row_out = pick(values, z, 1, 1)
    seen = [jnp.concatenate([row_out, pick(values, chol, wide, 1)], 1)]
    for s in range(n_chol - 1, 0, -1):
        seen.append(flip(jnp.concatenate([row_out, pick(values, chol ^ s, wide, 1)], 1), "chol", s))
    seen = jnp.concatenate(seen, 0)
    vecs = seen.shape[0]
    row_part, col_own = seen[:, :1].reshape(vecs, -1), seen[:, 1:].reshape(vecs, -1)

    col_got = lax.ppermute(seen[:, 1:], "core", SWAP).reshape(vecs, -1)
    head, flipped = head_product(row_part, col_own)
    return rest_product(head, flipped, col_own, col_got, span * orbitals)


def solution(mesh):
    n_ao, n_chol = mesh.shape["ao"], mesh.shape["chol"]
    split = Mesh(mesh.devices.reshape(n_ao // CORES, CORES, n_chol), (*AO, "chol"))
    placed = (P("chol", AO, None), P(AO, None))
    return jax.shard_map(
        body, mesh=split, in_specs=placed, out_specs=P(AO, "chol"), check_vma=False
    )
```

```python
import functools

import jax
import jax.numpy as jnp
from jax import lax
from jax.experimental import pallas as pl
from jax.experimental.layout import Layout, with_layout_constraint
from jax.experimental.pallas import tpu as pltpu
from jax.sharding import Mesh, PartitionSpec as P

CORES = 2
LAST = 2
AO = ("z", "core")
SWAP = [(0, 1), (1, 0)]


def pick(array, index, size, dim):
    return lax.dynamic_slice_in_dim(array, index * size, size, dim)


def row_major(array):
    return with_layout_constraint(array, Layout(tuple(range(array.ndim))))


def flip(array, axis, step):
    count = lax.axis_size(axis)
    return lax.ppermute(array, axis, [(d, d ^ step) for d in range(count)])


def project_kernel(parts, steps, *refs):
    lefts, held = refs[:parts], refs[parts : parts + len(steps)]
    before, out_ref = refs[parts + len(steps) : -1], refs[-1]
    z, core = lax.axis_index("z"), lax.axis_index("core")
    for p in range(out_ref.shape[0]):
        total = before[0][p] if before else 0.0
        for left_ref in lefts:
            for s, block_ref in zip(steps, held):
                total += lax.dot_general(
                    left_ref[p, z ^ s, core if left_ref.shape[2] > 1 else 0],
                    block_ref[...],
                    (((0,), (0,)), ((), ())),
                    preferred_element_type=jnp.float32,
                )
        out_ref[p] = total


def project(lefts, held, steps, *before, flops=None):
    vec_dev, nz, _, rows, orbitals = lefts[0].shape
    work = 2 * len(lefts) * len(steps) * vec_dev * rows * orbitals**2
    whole = pl.BlockSpec(memory_space=pltpu.VMEM)
    return pl.pallas_call(
        functools.partial(project_kernel, len(lefts), steps),
        out_shape=jax.ShapeDtypeStruct((vec_dev, orbitals, orbitals), jnp.float32),
        in_specs=[whole] * (len(lefts) + len(steps) + len(before)),
        out_specs=whole,
        compiler_params=pltpu.CompilerParams(vmem_limit_bytes=32 << 20),
        cost_estimate=pl.CostEstimate(
            flops=flops or work, bytes_accessed=(flops or work) // 1000, transcendentals=0
        ),
    )(*lefts, *[held[s] for s in steps], *before)


BLOCKS = 4


def block_product(flipped_ref, col_ref, into_ref, n, size):
    at = pl.ds(pl.multiple_of(n * size, size), size)
    return at, jnp.dot(
        flipped_ref[at, :], col_ref[...], preferred_element_type=jnp.float32
    ).astype(into_ref.dtype)


def head_kernel(size, row_ref, col_ref, head_ref, flipped_ref):
    flipped_ref[...] = row_ref[...].astype(jnp.float32).T.astype(flipped_ref.dtype)
    for n in range(head_ref.shape[0] // size):
        at, made = block_product(flipped_ref, col_ref, head_ref, n, size)
        head_ref[at, :] = made


def rest_kernel(side, size, head_ref, flipped_ref, own_ref, got_ref, out_ref, own, other, sems):
    core = lax.axis_index("core")
    parts = own_ref.shape[1] // side
    heads = head_ref.shape[0] // size

    def writes(source, n, to, owner):
        for part in range(parts):
            yield pltpu.make_async_copy(
                source.at[pl.ds(pl.multiple_of(n * size, size), size), pl.ds(part * side, side)],
                out_ref.at[
                    pl.ds(pl.multiple_of(to * size, size), size),
                    pl.ds(pl.multiple_of((part * CORES + owner) * side, side), side),
                ],
                sems.at[owner, to, part],
            )

    def each(act):
        for n in range(heads):
            for copy in writes(head_ref, n, n, core):
                act(copy)

        @pl.loop(0, BLOCKS - heads, unroll=act is start)
        def _(n):
            if act is start:
                to = n + heads
                made = block_product(flipped_ref, own_ref, own, to, size)[1]
                own[pl.ds(pl.multiple_of(n * size, size), size), :] = made
            for copy in writes(own, n, n + heads, core):
                act(copy)

        @pl.loop(0, BLOCKS, unroll=act is start)
        def _(n):
            if act is start:
                at, made = block_product(flipped_ref, got_ref, other, n, size)
                other[at, :] = made
            for copy in writes(other, n, n, 1 - core):
                act(copy)

    def start(copy):
        copy.start()

    each(start)
    each(lambda copy: copy.wait())


def head_product(row_part, col_part):
    vecs, rows = row_part.shape
    width = col_part.shape[1]
    whole = pl.BlockSpec(memory_space=pltpu.VMEM)
    return pl.pallas_call(
        functools.partial(head_kernel, rows // BLOCKS),
        out_shape=(
            jax.ShapeDtypeStruct((rows // 2, width), jnp.bfloat16),
            jax.ShapeDtypeStruct((rows, vecs), jnp.bfloat16),
        ),
        in_specs=[whole] * 2,
        out_specs=(whole, whole),
        compiler_params=pltpu.CompilerParams(vmem_limit_bytes=24 << 20),
        cost_estimate=pl.CostEstimate(
            flops=vecs * rows * width, bytes_accessed=rows * width, transcendentals=0
        ),
    )(row_part, col_part)


def rest_product(head, flipped, col_own, col_got, side):
    rows, vecs = flipped.shape
    width = col_own.shape[1]
    whole = pl.BlockSpec(memory_space=pltpu.VMEM)
    return pl.pallas_call(
        functools.partial(rest_kernel, side, rows // BLOCKS),
        out_shape=jax.ShapeDtypeStruct((rows, 2 * width), jnp.bfloat16),
        in_specs=[whole] * 4,
        out_specs=pl.BlockSpec(memory_space=pl.ANY),
        scratch_shapes=[
            pltpu.VMEM((rows - head.shape[0], width), jnp.bfloat16),
            pltpu.VMEM((rows, width), jnp.bfloat16),
            pltpu.SemaphoreType.DMA((CORES, BLOCKS, width // side)),
        ],
        compiler_params=pltpu.CompilerParams(vmem_limit_bytes=32 << 20),
        cost_estimate=pl.CostEstimate(
            flops=3 * vecs * rows * width, bytes_accessed=4 * rows * width, transcendentals=0
        ),
    )(head, flipped, col_own, col_got)


def body(cholesky, coeffs):
    vec_dev, rows, nao = cholesky.shape
    orbitals = coeffs.shape[1]
    nz, n_chol = lax.axis_size("z"), lax.axis_size("chol")
    z, core, chol = lax.axis_index("z"), lax.axis_index("core"), lax.axis_index("chol")

    held = [coeffs] + [flip(coeffs, "z", s) for s in range(1, nz)]

    left = jnp.einsum("ri,prk->pki", coeffs, cholesky, preferred_element_type=jnp.float32)
    left = left.astype(jnp.bfloat16).reshape(vec_dev, nz, CORES, rows, orbitals)
    give = lax.dynamic_slice_in_dim(left, 1 - core, 1, 2)
    got = lax.ppermute(give, "core", SWAP)
    late = LAST % nz
    steps = [s for s in range(nz) if s != late]
    partial = project([left], held, steps, flops=10**11)
    partial = project([got], held, steps, partial)
    partial = project([left, got], held, [late], partial)

    span = orbitals // (nz * CORES)
    partial = partial.reshape(vec_dev, nz, CORES, span, orbitals)
    total = lax.dynamic_index_in_dim(partial, core, 2, keepdims=False)
    total += lax.ppermute(
        lax.dynamic_index_in_dim(partial, 1 - core, 2, keepdims=False), "core", SWAP
    )
    rounded = total.astype(jnp.bfloat16)
    for s in range(1, nz):
        total += flip(rounded, "z", s).astype(jnp.float32)
    values = total.astype(jnp.bfloat16)

    wide = nz // n_chol
    row_out = pick(values, z, 1, 1)
    seen = [jnp.concatenate([row_out, pick(values, chol, wide, 1)], 1)]
    for s in range(n_chol - 1, 0, -1):
        seen.append(flip(jnp.concatenate([row_out, pick(values, chol ^ s, wide, 1)], 1), "chol", s))
    seen = row_major(jnp.concatenate(seen, 0))
    vecs = seen.shape[0]
    row_part, col_own = seen[:, :1].reshape(vecs, -1), seen[:, 1:].reshape(vecs, -1)

    col_got = lax.ppermute(seen[:, 1:], "core", SWAP).reshape(vecs, -1)
    head, flipped = head_product(row_part, col_own)
    return rest_product(head, flipped, col_own, col_got, span * orbitals)


def solution(mesh):
    n_ao, n_chol = mesh.shape["ao"], mesh.shape["chol"]
    split = Mesh(mesh.devices.reshape(n_ao // CORES, CORES, n_chol), (*AO, "chol"))
    placed = (P("chol", AO, None), P(AO, None))
    return jax.shard_map(
        body, mesh=split, in_specs=placed, out_specs=P(AO, "chol"), check_vma=False
    )
```

```python
import functools

import jax
import jax.numpy as jnp
from jax import lax
from jax.experimental import pallas as pl
from jax.experimental.layout import Layout, with_layout_constraint
from jax.experimental.pallas import tpu as pltpu
from jax.sharding import Mesh, PartitionSpec as P

CORES = 2
LATE = (1, 2)
AO = ("z", "core")
SWAP = [(0, 1), (1, 0)]


def pick(array, index, size, dim):
    return lax.dynamic_slice_in_dim(array, index * size, size, dim)


def row_major(array):
    return with_layout_constraint(array, Layout(tuple(range(array.ndim))))


def flip(array, axis, step):
    count = lax.axis_size(axis)
    return lax.ppermute(array, axis, [(d, d ^ step) for d in range(count)])


def project_kernel(parts, steps, *refs):
    lefts, held = refs[:parts], refs[parts : parts + len(steps)]
    before, out_ref = refs[parts + len(steps) : -1], refs[-1]
    z, core = lax.axis_index("z"), lax.axis_index("core")
    for p in range(out_ref.shape[0]):
        total = before[0][p] if before else 0.0
        for left_ref in lefts:
            for s, block_ref in zip(steps, held):
                total += lax.dot_general(
                    left_ref[p, z ^ s, core if left_ref.shape[2] > 1 else 0],
                    block_ref[...],
                    (((0,), (0,)), ((), ())),
                    preferred_element_type=jnp.float32,
                )
        out_ref[p] = total


def project(lefts, held, steps, *before, flops=None):
    vec_dev, nz, _, rows, orbitals = lefts[0].shape
    work = 2 * len(lefts) * len(steps) * vec_dev * rows * orbitals**2
    whole = pl.BlockSpec(memory_space=pltpu.VMEM)
    return pl.pallas_call(
        functools.partial(project_kernel, len(lefts), steps),
        out_shape=jax.ShapeDtypeStruct((vec_dev, orbitals, orbitals), jnp.float32),
        in_specs=[whole] * (len(lefts) + len(steps) + len(before)),
        out_specs=whole,
        compiler_params=pltpu.CompilerParams(vmem_limit_bytes=32 << 20),
        cost_estimate=pl.CostEstimate(
            flops=flops or work, bytes_accessed=(flops or work) // 1000, transcendentals=0
        ),
    )(*lefts, *[held[s] for s in steps], *before)


BLOCKS = 4


def block_product(flipped_ref, col_ref, into_ref, n, size):
    at = pl.ds(pl.multiple_of(n * size, size), size)
    return at, jnp.dot(
        flipped_ref[at, :], col_ref[...], preferred_element_type=jnp.float32
    ).astype(into_ref.dtype)


def head_kernel(size, row_ref, col_ref, head_ref, flipped_ref):
    flipped_ref[...] = row_ref[...].astype(jnp.float32).T.astype(flipped_ref.dtype)
    for n in range(head_ref.shape[0] // size):
        at, made = block_product(flipped_ref, col_ref, head_ref, n, size)
        head_ref[at, :] = made


def rest_kernel(side, size, head_ref, flipped_ref, own_ref, got_ref, out_ref, own, other, sems):
    core = lax.axis_index("core")
    parts = own_ref.shape[1] // side
    heads = head_ref.shape[0] // size

    def writes(source, n, to, owner):
        for part in range(parts):
            yield pltpu.make_async_copy(
                source.at[pl.ds(pl.multiple_of(n * size, size), size), pl.ds(part * side, side)],
                out_ref.at[
                    pl.ds(pl.multiple_of(to * size, size), size),
                    pl.ds(pl.multiple_of((part * CORES + owner) * side, side), side),
                ],
                sems.at[owner, to, part],
            )

    def each(act):
        for n in range(heads):
            for copy in writes(head_ref, n, n, core):
                act(copy)

        @pl.loop(0, BLOCKS - heads, unroll=act is start)
        def _(n):
            if act is start:
                to = n + heads
                made = block_product(flipped_ref, own_ref, own, to, size)[1]
                own[pl.ds(pl.multiple_of(n * size, size), size), :] = made
            for copy in writes(own, n, n + heads, core):
                act(copy)

        @pl.loop(0, BLOCKS, unroll=act is start)
        def _(n):
            if act is start:
                at, made = block_product(flipped_ref, got_ref, other, n, size)
                other[at, :] = made
            for copy in writes(other, n, n, 1 - core):
                act(copy)

    def start(copy):
        copy.start()

    each(start)
    each(lambda copy: copy.wait())


def head_product(row_part, col_part):
    vecs, rows = row_part.shape
    width = col_part.shape[1]
    whole = pl.BlockSpec(memory_space=pltpu.VMEM)
    return pl.pallas_call(
        functools.partial(head_kernel, rows // BLOCKS),
        out_shape=(
            jax.ShapeDtypeStruct((rows // 2, width), jnp.bfloat16),
            jax.ShapeDtypeStruct((rows, vecs), jnp.bfloat16),
        ),
        in_specs=[whole] * 2,
        out_specs=(whole, whole),
        compiler_params=pltpu.CompilerParams(vmem_limit_bytes=24 << 20),
        cost_estimate=pl.CostEstimate(
            flops=vecs * rows * width, bytes_accessed=rows * width, transcendentals=0
        ),
    )(row_part, col_part)


def rest_product(head, flipped, col_own, col_got, side):
    rows, vecs = flipped.shape
    width = col_own.shape[1]
    whole = pl.BlockSpec(memory_space=pltpu.VMEM)
    return pl.pallas_call(
        functools.partial(rest_kernel, side, rows // BLOCKS),
        out_shape=jax.ShapeDtypeStruct((rows, 2 * width), jnp.bfloat16),
        in_specs=[whole] * 4,
        out_specs=pl.BlockSpec(memory_space=pl.ANY),
        scratch_shapes=[
            pltpu.VMEM((rows - head.shape[0], width), jnp.bfloat16),
            pltpu.VMEM((rows, width), jnp.bfloat16),
            pltpu.SemaphoreType.DMA((CORES, BLOCKS, width // side)),
        ],
        compiler_params=pltpu.CompilerParams(vmem_limit_bytes=32 << 20),
        cost_estimate=pl.CostEstimate(
            flops=3 * vecs * rows * width, bytes_accessed=4 * rows * width, transcendentals=0
        ),
    )(head, flipped, col_own, col_got)


def body(cholesky, coeffs):
    vec_dev, rows, nao = cholesky.shape
    orbitals = coeffs.shape[1]
    nz, n_chol = lax.axis_size("z"), lax.axis_size("chol")
    z, core, chol = lax.axis_index("z"), lax.axis_index("core"), lax.axis_index("chol")

    held = [coeffs] + [flip(coeffs, "z", s) for s in range(1, nz)]

    left = jnp.einsum("ri,prk->pki", coeffs, cholesky, preferred_element_type=jnp.float32)
    left = left.astype(jnp.bfloat16).reshape(vec_dev, nz, CORES, rows, orbitals)
    give = lax.dynamic_slice_in_dim(left, 1 - core, 1, 2)
    got = lax.ppermute(give, "core", SWAP)
    late = [s for s in LATE if s < nz]
    steps = [s for s in range(nz) if s not in late]
    partial = project([left], held, steps, flops=10**11)
    partial = project([got], held, steps, partial)
    partial = project([left, got], held, late, partial)

    span = orbitals // (nz * CORES)
    partial = partial.reshape(vec_dev, nz, CORES, span, orbitals)
    total = lax.dynamic_index_in_dim(partial, core, 2, keepdims=False)
    total += lax.ppermute(
        lax.dynamic_index_in_dim(partial, 1 - core, 2, keepdims=False), "core", SWAP
    )
    rounded = total.astype(jnp.bfloat16)
    for s in range(1, nz):
        total += flip(rounded, "z", s).astype(jnp.float32)
    values = total.astype(jnp.bfloat16)

    wide = nz // n_chol
    row_out = pick(values, z, 1, 1)
    seen = [jnp.concatenate([row_out, pick(values, chol, wide, 1)], 1)]
    for s in range(n_chol - 1, 0, -1):
        seen.append(flip(jnp.concatenate([row_out, pick(values, chol ^ s, wide, 1)], 1), "chol", s))
    seen = row_major(jnp.concatenate(seen, 0))
    vecs = seen.shape[0]
    row_part, col_own = seen[:, :1].reshape(vecs, -1), seen[:, 1:].reshape(vecs, -1)

    col_got = lax.ppermute(seen[:, 1:], "core", SWAP).reshape(vecs, -1)
    head, flipped = head_product(row_part, col_own)
    return rest_product(head, flipped, col_own, col_got, span * orbitals)


def solution(mesh):
    n_ao, n_chol = mesh.shape["ao"], mesh.shape["chol"]
    split = Mesh(mesh.devices.reshape(n_ao // CORES, CORES, n_chol), (*AO, "chol"))
    placed = (P("chol", AO, None), P(AO, None))
    return jax.shard_map(
        body, mesh=split, in_specs=placed, out_specs=P(AO, "chol"), check_vma=False
    )
```

```python
import functools

import jax
import jax.numpy as jnp
from jax import lax
from jax.experimental import pallas as pl
from jax.experimental.layout import Layout, with_layout_constraint
from jax.experimental.pallas import tpu as pltpu
from jax.sharding import Mesh, PartitionSpec as P

CORES = 2
LATE = (1, 3)
AO = ("z", "core")
SWAP = [(0, 1), (1, 0)]


def pick(array, index, size, dim):
    return lax.dynamic_slice_in_dim(array, index * size, size, dim)


def row_major(array):
    return with_layout_constraint(array, Layout(tuple(range(array.ndim))))


def flip(array, axis, step):
    count = lax.axis_size(axis)
    return lax.ppermute(array, axis, [(d, d ^ step) for d in range(count)])


def project_kernel(parts, steps, *refs):
    lefts, held = refs[:parts], refs[parts : parts + len(steps)]
    before, out_ref = refs[parts + len(steps) : -1], refs[-1]
    z, core = lax.axis_index("z"), lax.axis_index("core")
    for p in range(out_ref.shape[0]):
        total = before[0][p] if before else 0.0
        for left_ref in lefts:
            for s, block_ref in zip(steps, held):
                total += lax.dot_general(
                    left_ref[p, z ^ s, core if left_ref.shape[2] > 1 else 0],
                    block_ref[...],
                    (((0,), (0,)), ((), ())),
                    preferred_element_type=jnp.float32,
                )
        out_ref[p] = total


def project(lefts, held, steps, *before, flops=None):
    vec_dev, nz, _, rows, orbitals = lefts[0].shape
    work = 2 * len(lefts) * len(steps) * vec_dev * rows * orbitals**2
    whole = pl.BlockSpec(memory_space=pltpu.VMEM)
    return pl.pallas_call(
        functools.partial(project_kernel, len(lefts), steps),
        out_shape=jax.ShapeDtypeStruct((vec_dev, orbitals, orbitals), jnp.float32),
        in_specs=[whole] * (len(lefts) + len(steps) + len(before)),
        out_specs=whole,
        compiler_params=pltpu.CompilerParams(vmem_limit_bytes=32 << 20),
        cost_estimate=pl.CostEstimate(
            flops=flops or work, bytes_accessed=(flops or work) // 1000, transcendentals=0
        ),
    )(*lefts, *[held[s] for s in steps], *before)


BLOCKS = 4


def block_product(flipped_ref, col_ref, into_ref, n, size):
    at = pl.ds(pl.multiple_of(n * size, size), size)
    return at, jnp.dot(
        flipped_ref[at, :], col_ref[...], preferred_element_type=jnp.float32
    ).astype(into_ref.dtype)


def head_kernel(size, row_ref, col_ref, head_ref, flipped_ref):
    flipped_ref[...] = row_ref[...].astype(jnp.float32).T.astype(flipped_ref.dtype)
    for n in range(head_ref.shape[0] // size):
        at, made = block_product(flipped_ref, col_ref, head_ref, n, size)
        head_ref[at, :] = made


def rest_kernel(side, size, head_ref, flipped_ref, own_ref, got_ref, out_ref, own, other, sems):
    core = lax.axis_index("core")
    parts = own_ref.shape[1] // side
    heads = head_ref.shape[0] // size

    def writes(source, n, to, owner):
        for part in range(parts):
            yield pltpu.make_async_copy(
                source.at[pl.ds(pl.multiple_of(n * size, size), size), pl.ds(part * side, side)],
                out_ref.at[
                    pl.ds(pl.multiple_of(to * size, size), size),
                    pl.ds(pl.multiple_of((part * CORES + owner) * side, side), side),
                ],
                sems.at[owner, to, part],
            )

    def each(act):
        for n in range(heads):
            for copy in writes(head_ref, n, n, core):
                act(copy)

        @pl.loop(0, BLOCKS - heads, unroll=act is start)
        def _(n):
            if act is start:
                to = n + heads
                made = block_product(flipped_ref, own_ref, own, to, size)[1]
                own[pl.ds(pl.multiple_of(n * size, size), size), :] = made
            for copy in writes(own, n, n + heads, core):
                act(copy)

        @pl.loop(0, BLOCKS, unroll=act is start)
        def _(n):
            if act is start:
                at, made = block_product(flipped_ref, got_ref, other, n, size)
                other[at, :] = made
            for copy in writes(other, n, n, 1 - core):
                act(copy)

    def start(copy):
        copy.start()

    each(start)
    each(lambda copy: copy.wait())


def head_product(row_part, col_part):
    vecs, rows = row_part.shape
    width = col_part.shape[1]
    whole = pl.BlockSpec(memory_space=pltpu.VMEM)
    return pl.pallas_call(
        functools.partial(head_kernel, rows // BLOCKS),
        out_shape=(
            jax.ShapeDtypeStruct((rows // 2, width), jnp.bfloat16),
            jax.ShapeDtypeStruct((rows, vecs), jnp.bfloat16),
        ),
        in_specs=[whole] * 2,
        out_specs=(whole, whole),
        compiler_params=pltpu.CompilerParams(vmem_limit_bytes=24 << 20),
        cost_estimate=pl.CostEstimate(
            flops=vecs * rows * width, bytes_accessed=rows * width, transcendentals=0
        ),
    )(row_part, col_part)


def rest_product(head, flipped, col_own, col_got, side):
    rows, vecs = flipped.shape
    width = col_own.shape[1]
    whole = pl.BlockSpec(memory_space=pltpu.VMEM)
    return pl.pallas_call(
        functools.partial(rest_kernel, side, rows // BLOCKS),
        out_shape=jax.ShapeDtypeStruct((rows, 2 * width), jnp.bfloat16),
        in_specs=[whole] * 4,
        out_specs=pl.BlockSpec(memory_space=pl.ANY),
        scratch_shapes=[
            pltpu.VMEM((rows - head.shape[0], width), jnp.bfloat16),
            pltpu.VMEM((rows, width), jnp.bfloat16),
            pltpu.SemaphoreType.DMA((CORES, BLOCKS, width // side)),
        ],
        compiler_params=pltpu.CompilerParams(vmem_limit_bytes=32 << 20),
        cost_estimate=pl.CostEstimate(
            flops=3 * vecs * rows * width, bytes_accessed=4 * rows * width, transcendentals=0
        ),
    )(head, flipped, col_own, col_got)


def body(cholesky, coeffs):
    vec_dev, rows, nao = cholesky.shape
    orbitals = coeffs.shape[1]
    nz, n_chol = lax.axis_size("z"), lax.axis_size("chol")
    z, core, chol = lax.axis_index("z"), lax.axis_index("core"), lax.axis_index("chol")

    held = [coeffs] + [flip(coeffs, "z", s) for s in range(1, nz)]

    left = jnp.einsum("ri,prk->pki", coeffs, cholesky, preferred_element_type=jnp.float32)
    left = left.astype(jnp.bfloat16).reshape(vec_dev, nz, CORES, rows, orbitals)
    give = lax.dynamic_slice_in_dim(left, 1 - core, 1, 2)
    got = lax.ppermute(give, "core", SWAP)
    late = [s for s in LATE if s < nz]
    steps = [s for s in range(nz) if s not in late]
    partial = project([left], held, steps, flops=10**11)
    partial = project([got], held, steps, partial)
    partial = project([left, got], held, late, partial)

    span = orbitals // (nz * CORES)
    partial = partial.reshape(vec_dev, nz, CORES, span, orbitals)
    total = lax.dynamic_index_in_dim(partial, core, 2, keepdims=False)
    total += lax.ppermute(
        lax.dynamic_index_in_dim(partial, 1 - core, 2, keepdims=False), "core", SWAP
    )
    rounded = total.astype(jnp.bfloat16)
    for s in range(1, nz):
        total += flip(rounded, "z", s).astype(jnp.float32)
    values = total.astype(jnp.bfloat16)

    wide = nz // n_chol
    row_out = pick(values, z, 1, 1)
    seen = [jnp.concatenate([row_out, pick(values, chol, wide, 1)], 1)]
    for s in range(n_chol - 1, 0, -1):
        seen.append(flip(jnp.concatenate([row_out, pick(values, chol ^ s, wide, 1)], 1), "chol", s))
    seen = row_major(jnp.concatenate(seen, 0))
    vecs = seen.shape[0]
    row_part, col_own = seen[:, :1].reshape(vecs, -1), seen[:, 1:].reshape(vecs, -1)

    col_got = lax.ppermute(seen[:, 1:], "core", SWAP).reshape(vecs, -1)
    head, flipped = head_product(row_part, col_own)
    return rest_product(head, flipped, col_own, col_got, span * orbitals)


def solution(mesh):
    n_ao, n_chol = mesh.shape["ao"], mesh.shape["chol"]
    split = Mesh(mesh.devices.reshape(n_ao // CORES, CORES, n_chol), (*AO, "chol"))
    placed = (P("chol", AO, None), P(AO, None))
    return jax.shard_map(
        body, mesh=split, in_specs=placed, out_specs=P(AO, "chol"), check_vma=False
    )
```

```python
import functools

import jax
import jax.numpy as jnp
from jax import lax
from jax.experimental import pallas as pl
from jax.experimental.layout import Layout, with_layout_constraint
from jax.experimental.pallas import tpu as pltpu
from jax.sharding import Mesh, PartitionSpec as P

CORES = 2
LAST = 2
AO = ("z", "core")
SWAP = [(0, 1), (1, 0)]


def pick(array, index, size, dim):
    return lax.dynamic_slice_in_dim(array, index * size, size, dim)


def row_major(array):
    return with_layout_constraint(array, Layout(tuple(range(array.ndim))))


def flip(array, axis, step):
    count = lax.axis_size(axis)
    return lax.ppermute(array, axis, [(d, d ^ step) for d in range(count)])


def project_kernel(parts, steps, *refs):
    lefts, held = refs[:parts], refs[parts : parts + len(steps)]
    before, out_ref = refs[parts + len(steps) : -1], refs[-1]
    z, core = lax.axis_index("z"), lax.axis_index("core")
    for p in range(out_ref.shape[0]):
        total = before[0][p] if before else 0.0
        for left_ref in lefts:
            for s, block_ref in zip(steps, held):
                total += lax.dot_general(
                    left_ref[p, z ^ s, core if left_ref.shape[2] > 1 else 0],
                    block_ref[...],
                    (((0,), (0,)), ((), ())),
                    preferred_element_type=jnp.float32,
                )
        out_ref[p] = total


def project(lefts, held, steps, *before, flops=None):
    vec_dev, nz, _, rows, orbitals = lefts[0].shape
    work = 2 * len(lefts) * len(steps) * vec_dev * rows * orbitals**2
    whole = pl.BlockSpec(memory_space=pltpu.VMEM)
    return pl.pallas_call(
        functools.partial(project_kernel, len(lefts), steps),
        out_shape=jax.ShapeDtypeStruct((vec_dev, orbitals, orbitals), jnp.float32),
        in_specs=[whole] * (len(lefts) + len(steps) + len(before)),
        out_specs=whole,
        compiler_params=pltpu.CompilerParams(vmem_limit_bytes=32 << 20),
        cost_estimate=pl.CostEstimate(
            flops=flops or work, bytes_accessed=(flops or work) // 1000, transcendentals=0
        ),
    )(*lefts, *[held[s] for s in steps], *before)


BLOCKS = 4


def block_product(flipped_ref, col_ref, into_ref, n, size):
    at = pl.ds(pl.multiple_of(n * size, size), size)
    return at, jnp.dot(
        flipped_ref[at, :], col_ref[...], preferred_element_type=jnp.float32
    ).astype(into_ref.dtype)


def head_kernel(size, row_ref, col_ref, head_ref, flipped_ref):
    flipped_ref[...] = row_ref[...].astype(jnp.float32).T.astype(flipped_ref.dtype)
    for n in range(head_ref.shape[0] // size):
        at, made = block_product(flipped_ref, col_ref, head_ref, n, size)
        head_ref[at, :] = made


def rest_kernel(side, size, head_ref, flipped_ref, own_ref, got_ref, out_ref, own, other, sems):
    core = lax.axis_index("core")
    parts = own_ref.shape[1] // side
    heads = head_ref.shape[0] // size

    def writes(source, n, to, owner):
        for part in range(parts):
            yield pltpu.make_async_copy(
                source.at[pl.ds(pl.multiple_of(n * size, size), size), pl.ds(part * side, side)],
                out_ref.at[
                    pl.ds(pl.multiple_of(to * size, size), size),
                    pl.ds(pl.multiple_of((part * CORES + owner) * side, side), side),
                ],
                sems.at[owner, to, part],
            )

    def each(act):
        for n in range(heads):
            for copy in writes(head_ref, n, n, core):
                act(copy)

        @pl.loop(0, BLOCKS - heads, unroll=act is start)
        def _(n):
            if act is start:
                to = n + heads
                made = block_product(flipped_ref, own_ref, own, to, size)[1]
                own[pl.ds(pl.multiple_of(n * size, size), size), :] = made
            for copy in writes(own, n, n + heads, core):
                act(copy)

        @pl.loop(0, BLOCKS, unroll=act is start)
        def _(n):
            if act is start:
                at, made = block_product(flipped_ref, got_ref, other, n, size)
                other[at, :] = made
            for copy in writes(other, n, n, 1 - core):
                act(copy)

    def start(copy):
        copy.start()

    each(start)
    each(lambda copy: copy.wait())


def head_product(row_part, col_part):
    vecs, rows = row_part.shape
    width = col_part.shape[1]
    whole = pl.BlockSpec(memory_space=pltpu.VMEM)
    return pl.pallas_call(
        functools.partial(head_kernel, rows // BLOCKS),
        out_shape=(
            jax.ShapeDtypeStruct((rows // 2, width), jnp.bfloat16),
            jax.ShapeDtypeStruct((rows, vecs), jnp.bfloat16),
        ),
        in_specs=[whole] * 2,
        out_specs=(whole, whole),
        compiler_params=pltpu.CompilerParams(vmem_limit_bytes=24 << 20),
        cost_estimate=pl.CostEstimate(
            flops=vecs * rows * width, bytes_accessed=rows * width, transcendentals=0
        ),
    )(row_part, col_part)


def rest_product(head, flipped, col_own, col_got, side):
    rows, vecs = flipped.shape
    width = col_own.shape[1]
    whole = pl.BlockSpec(memory_space=pltpu.VMEM)
    return pl.pallas_call(
        functools.partial(rest_kernel, side, rows // BLOCKS),
        out_shape=jax.ShapeDtypeStruct((rows, 2 * width), jnp.bfloat16),
        in_specs=[whole] * 4,
        out_specs=pl.BlockSpec(memory_space=pl.ANY),
        scratch_shapes=[
            pltpu.VMEM((rows - head.shape[0], width), jnp.bfloat16),
            pltpu.VMEM((rows, width), jnp.bfloat16),
            pltpu.SemaphoreType.DMA((CORES, BLOCKS, width // side)),
        ],
        compiler_params=pltpu.CompilerParams(vmem_limit_bytes=32 << 20),
        cost_estimate=pl.CostEstimate(
            flops=3 * vecs * rows * width, bytes_accessed=4 * rows * width, transcendentals=0
        ),
    )(head, flipped, col_own, col_got)


def body(cholesky, coeffs):
    vec_dev, rows, nao = cholesky.shape
    orbitals = coeffs.shape[1]
    nz, n_chol = lax.axis_size("z"), lax.axis_size("chol")
    z, core, chol = lax.axis_index("z"), lax.axis_index("core"), lax.axis_index("chol")

    held = [coeffs] + [flip(coeffs, "z", s) for s in range(1, nz)]

    left = jnp.einsum("ri,prk->pki", coeffs, cholesky, preferred_element_type=jnp.float32)
    left = left.astype(jnp.bfloat16).reshape(vec_dev, nz, CORES, rows, orbitals)
    give = lax.dynamic_slice_in_dim(left, 1 - core, 1, 2)
    got = lax.ppermute(give, "core", SWAP)
    late = LAST % nz
    steps = [s for s in range(nz) if s != late]
    partial = project([left], held, steps, flops=10**11)
    partial = project([got], held, steps, partial)
    partial = project([left, got], held, [late], partial)

    span = orbitals // (nz * CORES)
    partial = partial.reshape(vec_dev, nz, CORES, span, orbitals)
    total = lax.dynamic_index_in_dim(partial, core, 2, keepdims=False)
    total += lax.ppermute(
        lax.dynamic_index_in_dim(partial, 1 - core, 2, keepdims=False), "core", SWAP
    )
    rounded = total.astype(jnp.bfloat16)
    for s in (1, *range(nz - 1, 1, -1)):
        total += flip(rounded, "z", s).astype(jnp.float32)
    values = total.astype(jnp.bfloat16)

    wide = nz // n_chol
    row_out = pick(values, z, 1, 1)
    seen = [jnp.concatenate([row_out, pick(values, chol, wide, 1)], 1)]
    for s in range(n_chol - 1, 0, -1):
        seen.append(flip(jnp.concatenate([row_out, pick(values, chol ^ s, wide, 1)], 1), "chol", s))
    seen = row_major(jnp.concatenate(seen, 0))
    vecs = seen.shape[0]
    row_part, col_own = seen[:, :1].reshape(vecs, -1), seen[:, 1:].reshape(vecs, -1)

    col_got = lax.ppermute(seen[:, 1:], "core", SWAP).reshape(vecs, -1)
    head, flipped = head_product(row_part, col_own)
    return rest_product(head, flipped, col_own, col_got, span * orbitals)


def solution(mesh):
    n_ao, n_chol = mesh.shape["ao"], mesh.shape["chol"]
    split = Mesh(mesh.devices.reshape(n_ao // CORES, CORES, n_chol), (*AO, "chol"))
    placed = (P("chol", AO, None), P(AO, None))
    return jax.shard_map(
        body, mesh=split, in_specs=placed, out_specs=P(AO, "chol"), check_vma=False
    )
```

```python
import functools

import jax
import jax.numpy as jnp
from jax import lax
from jax.experimental import pallas as pl
from jax.experimental.layout import Layout, with_layout_constraint
from jax.experimental.pallas import tpu as pltpu
from jax.sharding import Mesh, PartitionSpec as P

CORES = 2
LAST = 2
AO = ("z", "core")
SWAP = [(0, 1), (1, 0)]


def pick(array, index, size, dim):
    return lax.dynamic_slice_in_dim(array, index * size, size, dim)


def row_major(array):
    return with_layout_constraint(array, Layout(tuple(range(array.ndim))))


def flip(array, axis, step):
    count = lax.axis_size(axis)
    return lax.ppermute(array, axis, [(d, d ^ step) for d in range(count)])


def project_kernel(parts, steps, *refs):
    lefts, held = refs[:parts], refs[parts : parts + len(steps)]
    before, out_ref = refs[parts + len(steps) : -1], refs[-1]
    z, core = lax.axis_index("z"), lax.axis_index("core")
    for p in range(out_ref.shape[0]):
        total = before[0][p] if before else 0.0
        for left_ref in lefts:
            for s, block_ref in zip(steps, held):
                total += lax.dot_general(
                    left_ref[p, z ^ s, core if left_ref.shape[2] > 1 else 0],
                    block_ref[...],
                    (((0,), (0,)), ((), ())),
                    preferred_element_type=jnp.float32,
                )
        out_ref[p] = total


def project(lefts, held, steps, *before, flops=None):
    vec_dev, nz, _, rows, orbitals = lefts[0].shape
    work = 2 * len(lefts) * len(steps) * vec_dev * rows * orbitals**2
    whole = pl.BlockSpec(memory_space=pltpu.VMEM)
    return pl.pallas_call(
        functools.partial(project_kernel, len(lefts), steps),
        out_shape=jax.ShapeDtypeStruct((vec_dev, orbitals, orbitals), jnp.float32),
        in_specs=[whole] * (len(lefts) + len(steps) + len(before)),
        out_specs=whole,
        compiler_params=pltpu.CompilerParams(vmem_limit_bytes=32 << 20),
        cost_estimate=pl.CostEstimate(
            flops=flops or work, bytes_accessed=(flops or work) // 1000, transcendentals=0
        ),
    )(*lefts, *[held[s] for s in steps], *before)


BLOCKS = 4


def block_product(flipped_ref, col_ref, into_ref, n, size):
    at = pl.ds(pl.multiple_of(n * size, size), size)
    return at, jnp.dot(
        flipped_ref[at, :], col_ref[...], preferred_element_type=jnp.float32
    ).astype(into_ref.dtype)


def head_kernel(size, row_ref, col_ref, head_ref, flipped_ref):
    flipped_ref[...] = row_ref[...].astype(jnp.float32).T.astype(flipped_ref.dtype)
    for n in range(head_ref.shape[0] // size):
        at, made = block_product(flipped_ref, col_ref, head_ref, n, size)
        head_ref[at, :] = made


def rest_kernel(side, size, head_ref, flipped_ref, own_ref, got_ref, out_ref, own, other, sems):
    core = lax.axis_index("core")
    parts = own_ref.shape[1] // side
    heads = head_ref.shape[0] // size

    def writes(source, n, to, owner):
        for part in range(parts):
            yield pltpu.make_async_copy(
                source.at[pl.ds(pl.multiple_of(n * size, size), size), pl.ds(part * side, side)],
                out_ref.at[
                    pl.ds(pl.multiple_of(to * size, size), size),
                    pl.ds(pl.multiple_of((part * CORES + owner) * side, side), side),
                ],
                sems.at[owner, to, part],
            )

    def each(act):
        for n in range(heads):
            for copy in writes(head_ref, n, n, core):
                act(copy)

        @pl.loop(0, BLOCKS - heads, unroll=act is start)
        def _(n):
            if act is start:
                to = n + heads
                made = block_product(flipped_ref, own_ref, own, to, size)[1]
                own[pl.ds(pl.multiple_of(n * size, size), size), :] = made
            for copy in writes(own, n, n + heads, core):
                act(copy)

        @pl.loop(0, BLOCKS, unroll=act is start)
        def _(n):
            if act is start:
                at, made = block_product(flipped_ref, got_ref, other, n, size)
                other[at, :] = made
            for copy in writes(other, n, n, 1 - core):
                act(copy)

    def start(copy):
        copy.start()

    each(start)
    each(lambda copy: copy.wait())


def head_product(row_part, col_part):
    vecs, rows = row_part.shape
    width = col_part.shape[1]
    whole = pl.BlockSpec(memory_space=pltpu.VMEM)
    return pl.pallas_call(
        functools.partial(head_kernel, rows // BLOCKS),
        out_shape=(
            jax.ShapeDtypeStruct((rows // 2, width), jnp.bfloat16),
            jax.ShapeDtypeStruct((rows, vecs), jnp.bfloat16),
        ),
        in_specs=[whole] * 2,
        out_specs=(whole, whole),
        compiler_params=pltpu.CompilerParams(vmem_limit_bytes=24 << 20),
        cost_estimate=pl.CostEstimate(
            flops=vecs * rows * width, bytes_accessed=rows * width, transcendentals=0
        ),
    )(row_part, col_part)


def rest_product(head, flipped, col_own, col_got, side):
    rows, vecs = flipped.shape
    width = col_own.shape[1]
    whole = pl.BlockSpec(memory_space=pltpu.VMEM)
    return pl.pallas_call(
        functools.partial(rest_kernel, side, rows // BLOCKS),
        out_shape=jax.ShapeDtypeStruct((rows, 2 * width), jnp.bfloat16),
        in_specs=[whole] * 4,
        out_specs=pl.BlockSpec(memory_space=pl.ANY),
        scratch_shapes=[
            pltpu.VMEM((rows - head.shape[0], width), jnp.bfloat16),
            pltpu.VMEM((rows, width), jnp.bfloat16),
            pltpu.SemaphoreType.DMA((CORES, BLOCKS, width // side)),
        ],
        compiler_params=pltpu.CompilerParams(vmem_limit_bytes=32 << 20),
        cost_estimate=pl.CostEstimate(
            flops=3 * vecs * rows * width, bytes_accessed=4 * rows * width, transcendentals=0
        ),
    )(head, flipped, col_own, col_got)


def body(cholesky, coeffs):
    vec_dev, rows, nao = cholesky.shape
    orbitals = coeffs.shape[1]
    nz, n_chol = lax.axis_size("z"), lax.axis_size("chol")
    z, core, chol = lax.axis_index("z"), lax.axis_index("core"), lax.axis_index("chol")

    held = [coeffs] + [flip(coeffs, "z", s) for s in range(1, nz)]

    left = jnp.einsum("ri,prk->pki", coeffs, cholesky, preferred_element_type=jnp.float32)
    left = left.astype(jnp.bfloat16).reshape(vec_dev, nz, CORES, rows, orbitals)
    give = lax.dynamic_slice_in_dim(left, 1 - core, 1, 2)
    got = lax.ppermute(give, "core", SWAP)
    late = LAST % nz
    steps = [s for s in range(nz) if s != late]
    partial = project([left], held, steps, flops=10**11)
    partial = project([got], held, steps, partial)
    partial = project([left, got], held, [late], partial)

    span = orbitals // (nz * CORES)
    partial = partial.reshape(vec_dev, nz, CORES, span, orbitals)
    total = lax.dynamic_index_in_dim(partial, core, 2, keepdims=False)
    total += lax.ppermute(
        lax.dynamic_index_in_dim(partial, 1 - core, 2, keepdims=False), "core", SWAP
    )
    rounded = total.astype(jnp.bfloat16)
    for s in (1, *range(nz - 1, 1, -1)):
        total += flip(rounded, "z", s).astype(jnp.float32)
    values = total.astype(jnp.bfloat16)

    wide = nz // n_chol
    row_out = pick(values, z, 1, 1)
    seen = [jnp.concatenate([row_out, pick(values, chol, wide, 1)], 1)]
    for s in (n_chol - 1, *range(1, n_chol - 1)):
        seen.append(flip(jnp.concatenate([row_out, pick(values, chol ^ s, wide, 1)], 1), "chol", s))
    seen = row_major(jnp.concatenate(seen, 0))
    vecs = seen.shape[0]
    row_part, col_own = seen[:, :1].reshape(vecs, -1), seen[:, 1:].reshape(vecs, -1)

    col_got = lax.ppermute(seen[:, 1:], "core", SWAP).reshape(vecs, -1)
    head, flipped = head_product(row_part, col_own)
    return rest_product(head, flipped, col_own, col_got, span * orbitals)


def solution(mesh):
    n_ao, n_chol = mesh.shape["ao"], mesh.shape["chol"]
    split = Mesh(mesh.devices.reshape(n_ao // CORES, CORES, n_chol), (*AO, "chol"))
    placed = (P("chol", AO, None), P(AO, None))
    return jax.shard_map(
        body, mesh=split, in_specs=placed, out_specs=P(AO, "chol"), check_vma=False
    )
```
